32 devices in a mesh: expert: 8 (over z, x), replica: 4 (over y, core).
Axes of the slice: x: 2, y: 2, z: 4, core: 2. Of those that a mesh axis runs over, the one named last changes fastest.
Arguments:
- grad_out: bfloat16 [4096, 2048], P(('expert', 'replica')), may hold values from -6 to 6
- gates: bfloat16 [4096, 8], P(('expert', 'replica')), may hold values from 0.019897461 to 0.5
- experts: int32 [4096, 8], P(('expert', 'replica')), may hold values from 0 to 31, all different within a row; in each aligned block of 128 rows (0 to 127, 128 to 255, ...) at most 80 rows name the same one
- hidden: bfloat16 [32, 4, 640, 768], P('expert', 'replica'), may hold values from -6 to 6
- down_weight: bfloat16 [2048, 32, 768], P(None, 'expert'), may hold values from -0.21875 to 0.21875
Outputs:
- d_hidden: bfloat16 [32, 4, 640, 768], P('expert', 'replica')
- d_down: bfloat16 [2048, 32, 768], P('replica', 'expert')
- d_gates: float32 [4096, 8], P(('expert', 'replica'))
The draws below stay inside these ranges and needn't reach their ends.
Inputs may be any that keep to these rules, and one draw needn't show every extreme that they name: Each token names 8 different experts. Among the 128 tokens of one device no expert is named by more than 80 tokens, a bound that some block reaches.
All inputs are finite; a program needn't handle non-finite values.
Results may differ from the reference program's by a relative error of at most 0.013.
Values may be sent and summed in bfloat16 or wider, within the bound.
No kernel may reach another device: no remote copies, remote signals or barrier semaphores. Data moves between devices by JAX's collectives and lax.ppermute only.
A program may use at most 192 MiB of HBM per device.

```python
import math
import jax
import jax.numpy as jnp
import numpy as np
from jax import lax

D = 2048
FF = 768
TOP = 8
TOK_DEV = 128
EXPERTS = 32
CAP = 80
SLOTS = 640
TOKENS = 4096
N_REPLICA = 4


def steps_of(own_key, extent, cuts, low, top_value):
    def one(dim, parts):
        draws = jax.random.uniform(jax.random.fold_in(jax.random.fold_in(own_key, 6), dim), (parts,), jnp.float32, low / len(cuts), top_value / len(cuts))
        return jnp.repeat(jnp.exp(draws), extent[dim] // parts).reshape((-1,) + (1,) * (len(extent) - dim - 1))

    loudness = one(*cuts[0])
    for cut in cuts[1:]:
        loudness = loudness * one(*cut)
    return loudness


def assign_block(rng, own, number, rows, amount, top, reach, skew):
    sequence = jax.random.permutation(rng, amount)
    heavy_load, ordinary = shares(amount, rows * top, reach, skew, True), shares(amount, rows * top, reach, skew, False)
    places = jnp.arange(amount)

    def named(tallies, offset_by):
        used = int((tallies > 0).sum())
        fixed = max(1, used // 4)
        passed = fixed + (places - fixed + offset_by * (used - fixed)) % max(1, amount - fixed)
        return jnp.zeros((amount,), jnp.int32).at[sequence[jnp.where(places < fixed, places, passed)]].set(jnp.asarray(tallies, jnp.int32))

    tallies = jnp.where(number % 4 == 0, named(heavy_load, number // 4), named(ordinary, number - number // 4 - 1))
    mixed = jax.random.permutation(jax.random.fold_in(own, 3), amount)
    donor, taker = mixed[0:amount // 2 * 2:2], mixed[1:amount // 2 * 2:2]
    margin = jnp.minimum(tallies[donor] - 1, reach - tallies[taker]) // 2
    margin = jnp.where((donor == sequence[0]) | (taker == sequence[0]) | (tallies[taker] == 0), 0, jnp.maximum(margin, 0))
    passed = jax.random.randint(jax.random.fold_in(own, 4), (amount // 2,), 0, 1 << 20) % (margin + 1)
    tallies = tallies.at[donor].add(-passed).at[taker].add(passed)
    items = jnp.searchsorted(jnp.cumsum(tallies), jnp.arange(rows * top), side="right").astype(jnp.int32)
    grid = items.reshape(top, rows).T
    grid = grid[jax.random.permutation(jax.random.fold_in(own, 1), rows)]
    offset_by = jax.random.randint(jax.random.fold_in(own, 2), (rows, 1), 0, top)
    return jnp.take_along_axis(grid, (jnp.arange(top)[None, :] + offset_by) % top, axis=1)


def shares(amount, total, most, slope, full):
    weights = [(1 << 20) // math.isqrt(grade ** slope) + 1 for grade in range(1, amount + 1)]
    largest = most if full else min(most, max(-(-total // amount), total * weights[0] // sum(weights)))
    least = 1 if total - largest >= amount - 1 else 0
    holding, surplus = [largest] + [least] * (amount - 1), total - largest - least * (amount - 1)
    while surplus > 0:
        free = [i for i in range(1, amount) if holding[i] < largest] or [i for i in range(1, amount) if holding[i] < most]
        whole, left = sum([weights[i] for i in free]), surplus
        for i in free:
            extra = min(most - holding[i], max(1, left * weights[i] // whole), surplus)
            holding[i] = holding[i] + extra
            surplus = surplus - extra
    return np.array(holding)


def normal_values(stream_key, shape, width, reach, shards=(), kind=jnp.bfloat16):
    result = width * jax.random.normal(stream_key, shape, jnp.float32)
    if shards:
        result = result * steps_of(stream_key, shape, shards, -0.22, 0.18)
    return jnp.clip(result, -reach, reach).astype(kind)


def setup_inputs(seed: int = 0) -> dict:
    key_of = jax.random.split(jax.random.key(seed), 6)
    grad_out = normal_values(key_of[0], (TOKENS, D), 1.0, 6.0, ((0, 32),))
    gates = jnp.clip(jnp.exp(math.log(0.5) - 3.224016 * jax.random.uniform(key_of[1], (TOKENS, TOP), jnp.float32) ** steps_of(key_of[1], (TOKENS, TOP), ((0, 32),), -0.2, 0.2)), 0.019897461, 0.5).astype(jnp.bfloat16)
    experts_keys = jax.random.split(jax.random.fold_in(key_of[2], 1), TOKENS // TOK_DEV)
    experts_turns = jax.random.permutation(jax.random.fold_in(key_of[2], 3), TOKENS // TOK_DEV)
    experts = jax.vmap(lambda own, number: assign_block(jax.random.fold_in(key_of[2], 2), own, number, TOK_DEV, EXPERTS, TOP, CAP, 2))(experts_keys, experts_turns).reshape((TOKENS, TOP))
    hidden = normal_values(key_of[3], (EXPERTS, N_REPLICA, SLOTS, FF), 1.0, 6.0, ((0, 8), (1, 4)))
    down_weight = normal_values(key_of[4], (D, EXPERTS, FF), FF ** -0.5, 0.21875, ((1, 8),))
    return {"grad_out": grad_out, "gates": gates, "experts": experts, "hidden": hidden, "down_weight": down_weight}


def reference(grad_out, gates, experts, hidden, down_weight):
    block_count = TOKENS // TOK_DEV
    pairs = experts.reshape(block_count, TOK_DEV * TOP)
    expert_range = jnp.arange(EXPERTS, dtype=jnp.int32)
    onehot_ids = (pairs[:, :, None] == expert_range[None, None, :]).astype(jnp.int32)
    running = jnp.cumsum(onehot_ids, axis=1)
    position = (jnp.sum(onehot_ids * running, axis=2) - 1).reshape(TOKENS, TOP)
    token_ids = jnp.arange(TOKENS, dtype=jnp.int32)
    block_ids = token_ids // TOK_DEV
    source_ids = block_ids // N_REPLICA
    replica_ids = block_ids % N_REPLICA
    slot_index = (experts * N_REPLICA + replica_ids[:, None]) * SLOTS + source_ids[:, None] * CAP + position
    slot_flat = slot_index.reshape(-1).astype(jnp.int32)
    total_rows = EXPERTS * N_REPLICA * SLOTS
    owner_ids = jnp.full((total_rows,), TOKENS, jnp.int32)
    owner_ids = owner_ids.at[slot_flat].set(jnp.broadcast_to(token_ids[:, None], (TOKENS, TOP)).reshape(-1))
    slot_gates = jnp.zeros((total_rows,), jnp.float32).at[slot_flat].set(gates.astype(jnp.float32).reshape(-1))
    owner_ids = owner_ids.reshape(EXPERTS, N_REPLICA * SLOTS)
    slot_gates = slot_gates.reshape(EXPERTS, N_REPLICA * SLOTS)
    padded = jnp.concatenate([grad_out, jnp.zeros((1, D), jnp.bfloat16)], axis=0)
    weights_by_expert = jnp.moveaxis(down_weight, 1, 0)

    def one_expert(inputs):
        owner_rows, gate_row, held, weight_matrix = inputs
        grad_slots = jnp.take(padded, owner_rows, axis=0)
        upstream = jnp.dot(grad_slots, weight_matrix, preferred_element_type=jnp.float32)
        held_values = held.reshape(N_REPLICA * SLOTS, FF).astype(jnp.float32)
        hidden_grad = (gate_row[:, None] * upstream).astype(jnp.bfloat16)
        slot_grad = jnp.sum(held_values * upstream, axis=1)
        weighted = (gate_row[:, None] * held_values).astype(jnp.bfloat16)
        weighted = weighted.reshape(N_REPLICA, SLOTS, FF).astype(jnp.float32)
        grad_parts = grad_slots.reshape(N_REPLICA, SLOTS, D).astype(jnp.float32)
        partials = jnp.einsum("rsf,rsd->rdf", weighted, grad_parts)
        rounded = lax.optimization_barrier(partials.astype(jnp.bfloat16))
        down_grad = jnp.sum(rounded.astype(jnp.float32), axis=0).astype(jnp.bfloat16)
        return hidden_grad.reshape(N_REPLICA, SLOTS, FF), slot_grad, down_grad

    hidden_grad, slot_grad, down_grad = lax.map(one_expert, (owner_ids, slot_gates, hidden, weights_by_expert))
    d_down = jnp.transpose(down_grad, (1, 0, 2))
    d_gates = jnp.take(slot_grad.reshape(-1), slot_flat, axis=0).reshape(TOKENS, TOP)
    return hidden_grad, d_down, d_gates
```

```python
import functools
import math

import jax
import jax.numpy as jnp
from jax import lax
from jax.experimental import pallas as pl
from jax.experimental.pallas import tpu as pltpu
from jax.sharding import PartitionSpec as P

FIRST_PARTS = (6, 4, 4, 3, 4, 3)
SECOND_PARTS = (6, 2)
BF16 = jnp.bfloat16
F32 = jnp.float32
MIB = 1024 * 1024
LITTLE = pl.CostEstimate(flops=1024, bytes_accessed=1024, transcendentals=0)


def info_of(offset, count):
    place, low, high = 0, 1, count // 2
    while high >= 1:
        place = place + (offset // high) % 2 * low
        low, high = low * 2, high // 2
    return place


def ring_place(index, count):
    return index // 2 if index % 2 == 0 else count - 1 - index // 2


def ring_index(place, count):
    return jnp.where(place < count // 2, 2 * place, 2 * (count - 1 - place) + 1)


def piece_of(source, place, count):
    ahead = (ring_place(source, count) + count - place) % count
    return jnp.where(ahead < count // 2, 2 * ahead, 2 * (count - ahead) - 1)


def source_of(piece, place, count):
    ahead = piece // 2 if piece % 2 == 0 else count - (piece + 1) // 2
    return ring_index((place + ahead) % count, count)


def turn_kernel(units, replicas, own_ref, grad_ref, *refs):
    outs, turned = refs[:-1], refs[-1]
    turned[...] = grad_ref[...].T
    rows = turned.shape[0] // replicas
    for out, parts in zip(outs, units):
        row = 0
        for flip, start, half in parts:
            for part in range(2):
                first = pl.multiple_of((own_ref[1] ^ (flip + part)) * rows + start, 128)
                out[row : row + half, :] = turned[pl.ds(first, half), :]
                row += half


def spread_kernel(
    count, own_ref, info_ref, hidden_ref, spread_ref, place_ref, gate_ref
):
    tokens, cap = spread_ref.shape[1], hidden_ref.shape[1] // count
    top = info_ref.shape[1] // 2
    me = own_ref[0]
    mine = me * pl.num_programs(0) + pl.program_id(0)
    masks, gates = [], []
    for source in range(count):
        info = info_ref[info_of(me ^ source, count)].astype(F32)
        same = info[:top].astype(jnp.int32) == mine
        masks.append(jnp.sum(jnp.where(same, 1.0, 0.0), axis=0, keepdims=True))
        gates.append(jnp.sum(jnp.where(same, info[top:], 0.0), axis=0, keepdims=True))
    mask, gate = jnp.concatenate(masks, axis=0), jnp.concatenate(gates, axis=0)
    before = lax.broadcasted_iota(jnp.int32, (tokens, tokens), 0)
    after = lax.broadcasted_iota(jnp.int32, (tokens, tokens), 1)
    earlier = jnp.where(before < after, 1.0, 0.0).astype(BF16)
    position = jnp.dot(mask.astype(BF16), earlier, preferred_element_type=F32)
    position = jnp.where(mask > 0.0, position, -1.0)
    base = lax.broadcasted_iota(jnp.int32, mask.shape, 0) * cap
    place_ref[0] = jnp.where(mask > 0.0, position.astype(jnp.int32) + base, -1)
    gate_ref[0] = gate
    turned = jnp.concatenate([position, gate], axis=0).T
    slot = lax.broadcasted_iota(jnp.int32, (tokens, cap), 1).astype(F32)
    for source in range(count):
        owns = turned[:, source : source + 1] == slot
        weights = jnp.where(owns, turned[:, count + source : count + source + 1], 0.0).astype(BF16)
        spread_ref[piece_of(source, own_ref[2], count)] = jnp.dot(
            weights, hidden_ref[0, source * cap : (source + 1) * cap, :], preferred_element_type=F32
        ).astype(BF16)


def down_kernel(first, count, *refs):
    piece_refs, spread_ref, outs, grads = refs[:count], refs[count], refs[count + 1 : -1], refs[-1]
    tokens, half = spread_ref.shape[1], grads.shape[0]

    @pl.when(pl.program_id(0) == 0)
    def _():
        for i, piece_ref in enumerate(piece_refs):
            grads[:, i * tokens : (i + 1) * tokens] = piece_ref[first : first + half, :]

    spread = spread_ref[...].reshape(count * tokens, spread_ref.shape[2])
    total = jnp.dot(grads[...], spread, preferred_element_type=F32)
    if outs[0].shape[0] == half and len(outs) > 1:
        total = total + outs[0][...].astype(F32)
        outs = outs[1:]
    row = 0
    for out in outs:
        out[...] = total[row : row + out.shape[0], :].astype(BF16)
        row += out.shape[0]


def up_kernel(units, replicas, count, own_ref, *refs):
    piece_refs, refs = refs[: len(units) * count], refs[len(units) * count :]
    weight_ref, place_ref, gate_ref, hidden_ref, hidden_grad_ref, slot_grad_ref, grads, placed = refs
    local, _, tokens = place_ref.shape
    slots = hidden_ref.shape[1]
    cap = slots // count
    group = 16 // math.gcd(cap, 16)
    rows = grads.shape[1] // replicas
    me, replica = own_ref[0], own_ref[1]
    expert = pl.program_id(0)

    def owned(x, low):
        slot = lax.broadcasted_iota(jnp.int32, (group * cap, tokens), 0) + low * cap
        return [place_ref[x, pl.ds(s, 1), :] == slot for s in range(low, low + group)]

    @pl.when(expert == 0)
    def _():
        for number, parts in enumerate(units):
            for i in range(count):
                turned = piece_refs[number * count + i][...].T
                token = pl.multiple_of(source_of(i, own_ref[2], count) * tokens, tokens)
                row = 0
                for flip, first, half in parts:
                    for part in range(2):
                        column = pl.multiple_of((replica ^ (flip + part)) * rows + first, 128)
                        grads[pl.ds(token, tokens), pl.ds(column, half)] = turned[:, row : row + half]
                        row += half
        for low in range(0, count, group):
            placing = jnp.concatenate(
                [
                    jnp.concatenate([jnp.where(o, 1.0, 0.0).astype(BF16) for o in owned(x, low)], axis=1)
                    for x in range(local)
                ],
                axis=0,
            )
            rows_there = jnp.dot(
                placing, grads[low * tokens : (low + group) * tokens, :], preferred_element_type=F32
            ).astype(BF16)
            for x in range(local):
                placed[x, low * cap : (low + group) * cap, :] = rows_there[
                    x * group * cap : (x + 1) * group * cap, :
                ]

    upstream = jnp.dot(placed[expert], weight_ref[0], preferred_element_type=F32)
    for low in range(0, count, group):
        slice_there = slice(low * cap, (low + group) * cap)
        mine = owned(expert, low)
        weighing = jnp.where(mine[0], gate_ref[expert, low : low + 1, :], 0.0)
        for s in range(1, group):
            weighing = weighing + jnp.where(mine[s], gate_ref[expert, low + s : low + s + 1, :], 0.0)
        gates = jnp.sum(weighing, axis=1, keepdims=True)
        part = upstream[slice_there, :]
        hidden_grad_ref[0, slice_there, :] = (gates * part).astype(BF16)
        slot_grad = jnp.sum(hidden_ref[0, slice_there, :].astype(F32) * part, axis=1, keepdims=True)
        for s in range(group):
            slot_grad_ref[0, pl.ds(me ^ (low + s), 1), :] = jnp.sum(
                jnp.where(mine[s], slot_grad, 0.0), axis=0, keepdims=True
            )


def join_kernel(near_ref, *refs):
    far_refs, out_ref = refs[: len(refs) - 1], refs[-1]
    local, width = out_ref.shape[1:]
    first = 0
    for far_ref in far_refs:
        if len(far_ref.shape) == 3:
            continue
        rows = pl.ds(first, far_ref.shape[0])
        total = near_ref[rows, :].astype(F32) + far_ref[...].astype(F32)
        for x in range(local):
            out_ref[rows, x, :] = total[:, x * width : (x + 1) * width].astype(BF16)
        first += far_ref.shape[0]


def tie(value, *others):
    return lax.optimization_barrier((value,) + others)[0]


SMEM = pl.BlockSpec(memory_space=pltpu.SMEM)


def whole(shape):
    return pl.BlockSpec(shape, lambda *_: (0,) * len(shape), pipeline_mode=pl.Buffered(1))


def vmem(shape):
    return pl.BlockSpec(shape, lambda *_: (0,) * len(shape))


def one_expert(*shape):
    return pl.BlockSpec((1,) + shape, lambda x: (x,) + (0,) * len(shape))


def per_device(grad_out, gates, experts, hidden, down_weight):
    count, replicas = lax.axis_size("expert"), lax.axis_size("replica")
    tokens, width = grad_out.shape
    top = experts.shape[1]
    local, _, slots, hidden_width = hidden.shape
    all_width = local * hidden_width
    rows = width // replicas
    hidden = hidden.reshape(local, slots, hidden_width)
    me = lax.axis_index("expert")
    place = jnp.where(me % 2 == 0, me // 2, count - 1 - me // 2)
    own = jnp.stack([me, lax.axis_index("replica"), place]).astype(jnp.int32)

    share = rows // (sum(FIRST_PARTS) + sum(SECOND_PARTS))
    half, second = share * sum(FIRST_PARTS), share * sum(SECOND_PARTS)
    units = (((2, 0, half),), ((2, half, second), (0, 0, rows)))
    unit_shapes = [
        jax.ShapeDtypeStruct((sum(2 * part[2] for part in parts), tokens), BF16) for parts in units
    ]
    sent = pl.pallas_call(
        functools.partial(turn_kernel, units, replicas),
        out_shape=unit_shapes,
        in_specs=[SMEM, vmem(grad_out.shape)],
        out_specs=[vmem(s.shape) for s in unit_shapes],
        scratch_shapes=[pltpu.VMEM((width, tokens), BF16)],
        compiler_params=pltpu.CompilerParams(vmem_limit_bytes=24 * MIB),
        name="turn_tokens",
    )(own, grad_out)
    info = jnp.concatenate([experts.T.astype(BF16), gates.T], axis=0)

    flips = []
    while 2 ** len(flips) < count:
        flips.insert(0, 2 ** len(flips))

    def hop(held, flip):
        moved = lax.ppermute(held, "expert", [(i, i ^ flip) for i in range(count)])
        return jnp.concatenate([held, moved], axis=0)

    ring = [i for i in range(0, count, 2)] + [i for i in range(count - 1, 0, -2)]
    onward = [(ring[i], ring[(i + 1) % count]) for i in range(count)]
    backward = [(b, a) for a, b in onward]

    def turn_ring(pieces):
        right, left = pieces[-2:] if len(pieces) > 1 else pieces * 2
        moved = [lax.ppermute(right, "expert", onward)]
        if len(pieces) + 1 < count:
            moved.append(lax.ppermute(left, "expert", backward))
        return moved

    def spread_hidden(infos):
        return pl.pallas_call(
            functools.partial(spread_kernel, count),
            grid=(local,),
            out_shape=[
                jax.ShapeDtypeStruct((count, tokens, all_width), BF16),
                jax.ShapeDtypeStruct((local, count, tokens), jnp.int32),
                jax.ShapeDtypeStruct((local, count, tokens), F32),
            ],
            in_specs=[SMEM, whole(infos.shape), one_expert(slots, hidden_width)],
            out_specs=[
                pl.BlockSpec((count, tokens, hidden_width), lambda x: (0, 0, x)),
                one_expert(count, tokens),
                one_expert(count, tokens),
            ],
            compiler_params=pltpu.CompilerParams(vmem_limit_bytes=24 * MIB),
            cost_estimate=LITTLE,
            name="spread_hidden",
        )(own, infos, hidden)

    def down(pieces, spread, first, half, parts=(1,), got=()):
        sizes = [half * part // sum(parts) for part in parts]

        def block(size):
            return pl.BlockSpec((size, hidden_width), lambda x: (0, x))

        return pl.pallas_call(
            functools.partial(down_kernel, first, count),
            grid=(local,),
            out_shape=[jax.ShapeDtypeStruct((size, all_width), BF16) for size in sizes],
            in_specs=[whole(piece.shape) for piece in pieces]
            + [pl.BlockSpec((count, tokens, hidden_width), lambda x: (0, 0, x))]
            + [block(half)] * len(got),
            out_specs=[block(size) for size in sizes],
            scratch_shapes=[pltpu.VMEM((half, count * tokens), BF16)],
            compiler_params=pltpu.CompilerParams(vmem_limit_bytes=24 * MIB),
            cost_estimate=LITTLE,
            name="down_grad",
        )(*pieces, spread, *got)

    def to_mate(give):
        return lax.ppermute(give, "replica", [(i, i ^ 1) for i in range(replicas)])

    def to_far(value):
        return lax.ppermute(value, "replica", [(i, i ^ 2) for i in range(replicas)])

    def up(pieces, weight, place, gate):
        return pl.pallas_call(
            functools.partial(up_kernel, units, replicas, count),
            grid=(local,),
            out_shape=[
                jax.ShapeDtypeStruct(hidden.shape, BF16),
                jax.ShapeDtypeStruct((local, count, tokens), F32),
            ],
            in_specs=[SMEM]
            + [whole(piece.shape) for piece in pieces]
            + [
                one_expert(width, hidden_width),
                whole(place.shape),
                whole(gate.shape),
                one_expert(slots, hidden_width),
            ],
            out_specs=[one_expert(slots, hidden_width), one_expert(count, tokens)],
            scratch_shapes=[
                pltpu.VMEM((count * tokens, width), BF16),
                pltpu.VMEM((local, slots, width), BF16),
            ],
            compiler_params=pltpu.CompilerParams(vmem_limit_bytes=48 * MIB),
            cost_estimate=LITTLE,
            name="hidden_grad",
        )(own, *pieces, weight, place, gate, hidden)

    def join(near, fars, first, *before):
        block = sum(far.shape[0] for far in fars)
        return pl.pallas_call(
            join_kernel,
            grid=(1,),
            out_shape=jax.ShapeDtypeStruct((rows, local, hidden_width), BF16),
            in_specs=[pl.BlockSpec((block, all_width), lambda i: (first // block, 0))]
            + [vmem(far.shape) for far in fars]
            + [pl.BlockSpec(memory_space=pl.ANY)] * len(before),
            out_specs=pl.BlockSpec((block, local, hidden_width), lambda i: (first // block, 0, 0)),
            input_output_aliases={1 + len(fars): 0} if before else {},
            compiler_params=pltpu.CompilerParams(vmem_limit_bytes=32 * MIB),
            cost_estimate=LITTLE,
            name="join",
        )(near, *fars, *before)

    step = lax.optimization_barrier
    infos = tie(info, sent[0])[None]
    first, rest = [sent[0]], [sent[1]]
    for number in range(count // 2):
        moved = turn_ring(first)
        if number < len(flips):
            infos = hop(infos, flips[number])
        if number + 1 < count // 2:
            infos, rest[0], *first = step((infos, rest[0], *first, *moved))
        else:
            first = [*first, *moved]
    for flip in flips[count // 2 :]:
        infos = hop(infos, flip)
    spread, place, gate = spread_hidden(infos)
    spread, *first = step((spread, *first))

    def pass_on(returned, flip):
        stay = returned.reshape(count // (2 * flip), 2, flip, local, tokens)
        moved = lax.ppermute(stay[:, 1], "expert", [(i, i ^ flip) for i in range(count)])
        return jnp.stack([stay[:, 0], moved], axis=1).reshape(count, local, tokens)

    moved = turn_ring(rest)
    (give,) = down(first, spread, half, half)
    give, *rest = step((give, *rest, *moved))
    moved = turn_ring(rest)
    parts = list(down(first, spread, 0, half, FIRST_PARTS, (to_mate(give),)))
    *parts, spread = step((*parts, spread))
    rest = list(step((*rest, *moved)))
    weight = jnp.transpose(tie(down_weight, rest[-1]), (1, 0, 2))
    far_first = [to_far(parts[0])]
    while len(rest) < count:
        moved = turn_ring(rest)
        sent_now = len(far_first) < 3
        if sent_now:
            far_first.append(to_far(parts[len(far_first)]))
            far_first[-2], weight, *rest = step((far_first[-2], weight, *rest, *moved))
        else:
            weight, *rest = step((weight, *rest, *moved))

    far_first.append(to_far(parts[3]))
    (give,) = down(rest, spread, second, second)
    far_first[2], give, spread, *parts = step((far_first[2], give, spread, *parts))
    (own_give,) = down(rest, spread, 2 * second + rows, rows)
    far_first[3], got, own_give, *parts = step((far_first[3], to_mate(give), own_give, *parts))
    far_first.append(to_far(parts[4]))
    sums = down(rest, spread, 0, second, SECOND_PARTS, (got,))
    spread = tie(spread, *sums)
    (near,) = down(rest, spread, 2 * second, rows, (1,), (to_mate(own_give),))
    far_first[4], near, place, *sums = step((far_first[4], near, place, *sums, *parts))[: 3 + len(sums)]
    far_first.append(to_far(parts[5]))
    far_second = [to_far(sums[0])]
    hidden_grad, slot_grad = up(first + rest, weight, place, gate)
    far_first[5], far_second[0], hidden_grad, slot_grad, near = step(
        (far_first[5], far_second[0], hidden_grad, slot_grad, near)
    )
    far_second.append(to_far(sums[1]))

    returned = pass_on(jnp.transpose(slot_grad, (1, 0, 2)), flips[0])
    down_grad = join(near, far_first, 0)
    far_second[1], returned, down_grad = step((far_second[1], returned, down_grad))
    for flip in flips[1:]:
        returned = pass_on(returned, flip)
    down_grad = join(near, far_second, half, down_grad)
    sources = lax.axis_index("expert").astype(jnp.int32) ^ jnp.arange(count, dtype=jnp.int32)
    numbers = (sources[:, None] * local + jnp.arange(local, dtype=jnp.int32)[None]).reshape(-1)
    named = experts.T[:, None, :] == numbers[None, :, None]
    gate_grad = jnp.sum(jnp.where(named, returned.reshape(1, -1, tokens), 0.0), axis=1).T

    return hidden_grad.reshape(local, 1, slots, hidden_width), down_grad, gate_grad


def solution(mesh):
    in_specs = (
        P(("expert", "replica"), None),
        P(("expert", "replica"), None),
        P(("expert", "replica"), None),
        P("expert", "replica", None, None),
        P(None, "expert", None),
    )
    out_specs = (
        P("expert", "replica", None, None),
        P("replica", "expert", None),
        P(("expert", "replica"), None),
    )
    return jax.shard_map(
        per_device, mesh=mesh, in_specs=in_specs, out_specs=out_specs, check_vma=False
    )
```

```python
import functools
import math

import jax
import jax.numpy as jnp
from jax import lax
from jax.experimental import pallas as pl
from jax.experimental.pallas import tpu as pltpu
from jax.sharding import PartitionSpec as P

FIRST_PARTS = (6, 4, 3, 3)
SECOND_PARTS = (8, 4, 4)
BF16 = jnp.bfloat16
F32 = jnp.float32
MIB = 1024 * 1024
LITTLE = pl.CostEstimate(flops=1024, bytes_accessed=1024, transcendentals=0)


def info_of(offset, count):
    place, low, high = 0, 1, count // 2
    while high >= 1:
        place = place + (offset // high) % 2 * low
        low, high = low * 2, high // 2
    return place


def ring_place(index, count):
    return index // 2 if index % 2 == 0 else count - 1 - index // 2


def ring_index(place, count):
    return jnp.where(place < count // 2, 2 * place, 2 * (count - 1 - place) + 1)


def piece_of(source, place, count):
    ahead = (ring_place(source, count) + count - place) % count
    return jnp.where(ahead < count // 2, 2 * ahead, 2 * (count - ahead) - 1)


def source_of(piece, place, count):
    ahead = piece // 2 if piece % 2 == 0 else count - (piece + 1) // 2
    return ring_index((place + ahead) % count, count)


def turn_kernel(units, replicas, own_ref, grad_ref, *refs):
    outs, turned = refs[:-1], refs[-1]
    turned[...] = grad_ref[...].T
    rows = turned.shape[0] // replicas
    for out, parts in zip(outs, units):
        row = 0
        for flip, start, half in parts:
            for part in range(2):
                first = pl.multiple_of((own_ref[1] ^ (flip + part)) * rows + start, 128)
                out[row : row + half, :] = turned[pl.ds(first, half), :]
                row += half


def spread_kernel(
    count, own_ref, info_ref, hidden_ref, spread_ref, place_ref, gate_ref
):
    tokens, cap = spread_ref.shape[1], hidden_ref.shape[1] // count
    top = info_ref.shape[1] // 2
    me = own_ref[0]
    mine = me * pl.num_programs(0) + pl.program_id(0)
    masks, gates = [], []
    for source in range(count):
        info = info_ref[info_of(me ^ source, count)].astype(F32)
        same = info[:top].astype(jnp.int32) == mine
        masks.append(jnp.sum(jnp.where(same, 1.0, 0.0), axis=0, keepdims=True))
        gates.append(jnp.sum(jnp.where(same, info[top:], 0.0), axis=0, keepdims=True))
    mask, gate = jnp.concatenate(masks, axis=0), jnp.concatenate(gates, axis=0)
    before = lax.broadcasted_iota(jnp.int32, (tokens, tokens), 0)
    after = lax.broadcasted_iota(jnp.int32, (tokens, tokens), 1)
    earlier = jnp.where(before < after, 1.0, 0.0).astype(BF16)
    position = jnp.dot(mask.astype(BF16), earlier, preferred_element_type=F32)
    position = jnp.where(mask > 0.0, position, -1.0)
    base = lax.broadcasted_iota(jnp.int32, mask.shape, 0) * cap
    place_ref[0] = jnp.where(mask > 0.0, position.astype(jnp.int32) + base, -1)
    gate_ref[0] = gate
    turned = jnp.concatenate([position, gate], axis=0).T
    slot = lax.broadcasted_iota(jnp.int32, (tokens, cap), 1).astype(F32)
    for source in range(count):
        owns = turned[:, source : source + 1] == slot
        weights = jnp.where(owns, turned[:, count + source : count + source + 1], 0.0).astype(BF16)
        spread_ref[piece_of(source, own_ref[2], count)] = jnp.dot(
            weights, hidden_ref[0, source * cap : (source + 1) * cap, :], preferred_element_type=F32
        ).astype(BF16)


def down_kernel(first, count, *refs):
    piece_refs, spread_ref, outs, grads = refs[:count], refs[count], refs[count + 1 : -1], refs[-1]
    tokens, half = spread_ref.shape[1], grads.shape[0]

    @pl.when(pl.program_id(0) == 0)
    def _():
        for i, piece_ref in enumerate(piece_refs):
            grads[:, i * tokens : (i + 1) * tokens] = piece_ref[first : first + half, :]

    spread = spread_ref[...].reshape(count * tokens, spread_ref.shape[2])
    total = jnp.dot(grads[...], spread, preferred_element_type=F32)
    if outs[0].shape[0] == half and len(outs) > 1:
        total = total + outs[0][...].astype(F32)
        outs = outs[1:]
    row = 0
    for out in outs:
        out[...] = total[row : row + out.shape[0], :].astype(BF16)
        row += out.shape[0]


def up_kernel(units, replicas, count, own_ref, *refs):
    piece_refs, refs = refs[: len(units) * count], refs[len(units) * count :]
    weight_ref, place_ref, gate_ref, hidden_ref, hidden_grad_ref, slot_grad_ref, grads, placed = refs
    local, _, tokens = place_ref.shape
    slots = hidden_ref.shape[1]
    cap = slots // count
    group = 16 // math.gcd(cap, 16)
    rows = grads.shape[1] // replicas
    me, replica = own_ref[0], own_ref[1]
    expert = pl.program_id(0)

    def owned(x, low):
        slot = lax.broadcasted_iota(jnp.int32, (group * cap, tokens), 0) + low * cap
        return [place_ref[x, pl.ds(s, 1), :] == slot for s in range(low, low + group)]

    @pl.when(expert == 0)
    def _():
        for number, parts in enumerate(units):
            for i in range(count):
                turned = piece_refs[number * count + i][...].T
                token = pl.multiple_of(source_of(i, own_ref[2], count) * tokens, tokens)
                row = 0
                for flip, first, half in parts:
                    for part in range(2):
                        column = pl.multiple_of((replica ^ (flip + part)) * rows + first, 128)
                        grads[pl.ds(token, tokens), pl.ds(column, half)] = turned[:, row : row + half]
                        row += half
        for low in range(0, count, group):
            placing = jnp.concatenate(
                [
                    jnp.concatenate([jnp.where(o, 1.0, 0.0).astype(BF16) for o in owned(x, low)], axis=1)
                    for x in range(local)
                ],
                axis=0,
            )
            rows_there = jnp.dot(
                placing, grads[low * tokens : (low + group) * tokens, :], preferred_element_type=F32
            ).astype(BF16)
            for x in range(local):
                placed[x, low * cap : (low + group) * cap, :] = rows_there[
                    x * group * cap : (x + 1) * group * cap, :
                ]

    upstream = jnp.dot(placed[expert], weight_ref[0], preferred_element_type=F32)
    for low in range(0, count, group):
        slice_there = slice(low * cap, (low + group) * cap)
        mine = owned(expert, low)
        weighing = jnp.where(mine[0], gate_ref[expert, low : low + 1, :], 0.0)
        for s in range(1, group):
            weighing = weighing + jnp.where(mine[s], gate_ref[expert, low + s : low + s + 1, :], 0.0)
        gates = jnp.sum(weighing, axis=1, keepdims=True)
        part = upstream[slice_there, :]
        hidden_grad_ref[0, slice_there, :] = (gates * part).astype(BF16)
        slot_grad = jnp.sum(hidden_ref[0, slice_there, :].astype(F32) * part, axis=1, keepdims=True)
        for s in range(group):
            slot_grad_ref[0, pl.ds(me ^ (low + s), 1), :] = jnp.sum(
                jnp.where(mine[s], slot_grad, 0.0), axis=0, keepdims=True
            )


def join_kernel(near_ref, *refs):
    far_refs, out_ref = refs[: len(refs) - 1], refs[-1]
    local, width = out_ref.shape[1:]
    first = 0
    for far_ref in far_refs:
        if len(far_ref.shape) == 3:
            continue
        rows = pl.ds(first, far_ref.shape[0])
        total = near_ref[rows, :].astype(F32) + far_ref[...].astype(F32)
        for x in range(local):
            out_ref[rows, x, :] = total[:, x * width : (x + 1) * width].astype(BF16)
        first += far_ref.shape[0]


def tie(value, *others):
    return lax.optimization_barrier((value,) + others)[0]


SMEM = pl.BlockSpec(memory_space=pltpu.SMEM)


def whole(shape):
    return pl.BlockSpec(shape, lambda *_: (0,) * len(shape), pipeline_mode=pl.Buffered(1))


def vmem(shape):
    return pl.BlockSpec(shape, lambda *_: (0,) * len(shape))


def one_expert(*shape):
    return pl.BlockSpec((1,) + shape, lambda x: (x,) + (0,) * len(shape))


def per_device(grad_out, gates, experts, hidden, down_weight):
    count, replicas = lax.axis_size("expert"), lax.axis_size("replica")
    tokens, width = grad_out.shape
    top = experts.shape[1]
    local, _, slots, hidden_width = hidden.shape
    all_width = local * hidden_width
    room = min(max(2 * count, 16), 56)
    rows = width // replicas
    hidden = hidden.reshape(local, slots, hidden_width)
    me = lax.axis_index("expert")
    place = jnp.where(me % 2 == 0, me // 2, count - 1 - me // 2)
    own = jnp.stack([me, lax.axis_index("replica"), place]).astype(jnp.int32)

    share = rows // (sum(FIRST_PARTS) + sum(SECOND_PARTS))
    half, second = share * sum(FIRST_PARTS), share * sum(SECOND_PARTS)
    units = (((2, 0, half),), ((2, half, second), (0, 0, rows)))
    unit_shapes = [
        jax.ShapeDtypeStruct((sum(2 * part[2] for part in parts), tokens), BF16) for parts in units
    ]
    sent = pl.pallas_call(
        functools.partial(turn_kernel, units, replicas),
        out_shape=unit_shapes,
        in_specs=[SMEM, vmem(grad_out.shape)],
        out_specs=[vmem(s.shape) for s in unit_shapes],
        scratch_shapes=[pltpu.VMEM((width, tokens), BF16)],
        compiler_params=pltpu.CompilerParams(vmem_limit_bytes=56 * MIB),
        name="turn_tokens",
    )(own, grad_out)
    info = jnp.concatenate([experts.T.astype(BF16), gates.T], axis=0)

    flips = []
    while 2 ** len(flips) < count:
        flips.insert(0, 2 ** len(flips))

    def hop(held, flip):
        moved = lax.ppermute(held, "expert", [(i, i ^ flip) for i in range(count)])
        return jnp.concatenate([held, moved], axis=0)

    ring = [i for i in range(0, count, 2)] + [i for i in range(count - 1, 0, -2)]
    onward = [(ring[i], ring[(i + 1) % count]) for i in range(count)]
    backward = [(b, a) for a, b in onward]

    def turn_ring(pieces):
        right, left = pieces[-2:] if len(pieces) > 1 else pieces * 2
        moved = [lax.ppermute(right, "expert", onward)]
        if len(pieces) + 1 < count:
            moved.append(lax.ppermute(left, "expert", backward))
        return moved

    def spread_hidden(infos):
        return pl.pallas_call(
            functools.partial(spread_kernel, count),
            grid=(local,),
            out_shape=[
                jax.ShapeDtypeStruct((count, tokens, all_width), BF16),
                jax.ShapeDtypeStruct((local, count, tokens), jnp.int32),
                jax.ShapeDtypeStruct((local, count, tokens), F32),
            ],
            in_specs=[SMEM, whole(infos.shape), one_expert(slots, hidden_width)],
            out_specs=[
                pl.BlockSpec((count, tokens, hidden_width), lambda x: (0, 0, x)),
                one_expert(count, tokens),
                one_expert(count, tokens),
            ],
            compiler_params=pltpu.CompilerParams(vmem_limit_bytes=room * MIB),
            cost_estimate=LITTLE,
            name="spread_hidden",
        )(own, infos, hidden)

    def down(pieces, spread, first, half, parts=(1,), got=()):
        sizes = [half * part // sum(parts) for part in parts]

        def block(size):
            return pl.BlockSpec((size, hidden_width), lambda x: (0, x))

        return pl.pallas_call(
            functools.partial(down_kernel, first, count),
            grid=(local,),
            out_shape=[jax.ShapeDtypeStruct((size, all_width), BF16) for size in sizes],
            in_specs=[whole(piece.shape) for piece in pieces]
            + [pl.BlockSpec((count, tokens, hidden_width), lambda x: (0, 0, x))]
            + [block(half)] * len(got),
            out_specs=[block(size) for size in sizes],
            scratch_shapes=[pltpu.VMEM((half, count * tokens), BF16)],
            compiler_params=pltpu.CompilerParams(vmem_limit_bytes=room * MIB),
            cost_estimate=LITTLE,
            name="down_grad",
        )(*pieces, spread, *got)

    def to_mate(give):
        return lax.ppermute(give, "replica", [(i, i ^ 1) for i in range(replicas)])

    def to_far(value):
        return lax.ppermute(value, "replica", [(i, i ^ 2) for i in range(replicas)])

    def up(pieces, weight, place, gate):
        return pl.pallas_call(
            functools.partial(up_kernel, units, replicas, count),
            grid=(local,),
            out_shape=[
                jax.ShapeDtypeStruct(hidden.shape, BF16),
                jax.ShapeDtypeStruct((local, count, tokens), F32),
            ],
            in_specs=[SMEM]
            + [whole(piece.shape) for piece in pieces]
            + [
                one_expert(width, hidden_width),
                whole(place.shape),
                whole(gate.shape),
                one_expert(slots, hidden_width),
            ],
            out_specs=[one_expert(slots, hidden_width), one_expert(count, tokens)],
            scratch_shapes=[
                pltpu.VMEM((count * tokens, width), BF16),
                pltpu.VMEM((local, slots, width), BF16),
            ],
            compiler_params=pltpu.CompilerParams(vmem_limit_bytes=min(5 * count, 58) * MIB),
            cost_estimate=LITTLE,
            name="hidden_grad",
        )(own, *pieces, weight, place, gate, hidden)

    def join(near, fars, first, *before):
        block = sum(far.shape[0] for far in fars)
        return pl.pallas_call(
            join_kernel,
            grid=(1,),
            out_shape=jax.ShapeDtypeStruct((rows, local, hidden_width), BF16),
            in_specs=[pl.BlockSpec((block, all_width), lambda i: (first // block, 0))]
            + [vmem(far.shape) for far in fars]
            + [pl.BlockSpec(memory_space=pl.ANY)] * len(before),
            out_specs=pl.BlockSpec((block, local, hidden_width), lambda i: (first // block, 0, 0)),
            input_output_aliases={1 + len(fars): 0} if before else {},
            compiler_params=pltpu.CompilerParams(vmem_limit_bytes=24 * MIB),
            cost_estimate=LITTLE,
            name="join",
        )(near, *fars, *before)

    step = lax.optimization_barrier
    infos = tie(info, sent[0])[None]
    first, rest = [sent[0]], [sent[1]]
    for number in range(count // 2):
        moved = turn_ring(first)
        if number < len(flips):
            infos = hop(infos, flips[number])
        if number + 1 < count // 2:
            infos, rest[0], *first = step((infos, rest[0], *first, *moved))
        else:
            first = [*first, *moved]
    for flip in flips[count // 2 :]:
        infos = hop(infos, flip)
    spread, place, gate = spread_hidden(infos)
    spread, *first = step((spread, *first))

    def pass_on(returned, flip):
        stay = returned.reshape(count // (2 * flip), 2, flip, local, tokens)
        moved = lax.ppermute(stay[:, 1], "expert", [(i, i ^ flip) for i in range(count)])
        return jnp.stack([stay[:, 0], moved], axis=1).reshape(count, local, tokens)

    moved = turn_ring(rest)
    (give,) = down(first, spread, half, half)
    give, *rest = step((give, *rest, *moved))
    moved = turn_ring(rest)
    parts = list(down(first, spread, 0, half, FIRST_PARTS, (to_mate(give),)))
    *parts, spread = step((*parts, spread))
    rest = list(step((*rest, *moved)))
    weight = jnp.transpose(tie(down_weight, rest[-1]), (1, 0, 2))
    far_first = [to_far(part) for part in parts[:3]]
    moved = turn_ring(rest)
    far_first[0], weight, *rest = step((far_first[0], weight, *rest, *moved))
    while len(rest) < count:
        moved = turn_ring(rest)
        far_first[1], *rest = step((far_first[1], *rest, *moved))

    (give,) = down(rest, spread, second, second)
    far_first[2], give, spread, *parts = step((far_first[2], give, spread, *parts))
    far_first.append(to_far(parts[3]))
    (own_give,) = down(rest, spread, 2 * second + rows, rows)
    far_first[3], got, own_give, spread = step((far_first[3], to_mate(give), own_give, spread))
    sums = down(rest, spread, 0, second, SECOND_PARTS, (got,))
    (near,) = down(rest, tie(spread, *sums), 2 * second, rows, (1,), (to_mate(own_give),))
    near, place = step((near, place))
    far_second = [to_far(part) for part in sums]
    hidden_grad, slot_grad = up(first + rest, weight, place, gate)
    far_second[0], hidden_grad, slot_grad, near = step((far_second[0], hidden_grad, slot_grad, near))

    returned = pass_on(jnp.transpose(slot_grad, (1, 0, 2)), flips[0])
    down_grad = join(near, far_first, 0)
    far_second[1], returned, down_grad = step((far_second[1], returned, down_grad))
    returned = pass_on(returned, flips[1])
    down_grad = join(near, far_second[:1], half, down_grad)
    far_second[2], returned, down_grad = step((far_second[2], returned, down_grad))
    for flip in flips[2:]:
        returned = pass_on(returned, flip)
    sources = lax.axis_index("expert").astype(jnp.int32) ^ jnp.arange(count, dtype=jnp.int32)
    numbers = (sources[:, None] * local + jnp.arange(local, dtype=jnp.int32)[None]).reshape(-1)
    named = experts.T[:, None, :] == numbers[None, :, None]
    gate_grad = jnp.sum(jnp.where(named, returned.reshape(1, -1, tokens), 0.0), axis=1)
    gate_grad = gate_grad.T
    down_grad = join(near, far_second[1:], rows - sum(far.shape[0] for far in far_second[1:]), down_grad)
    return hidden_grad.reshape(local, 1, slots, hidden_width), down_grad, gate_grad


def solution(mesh):
    in_specs = (
        P(("expert", "replica"), None),
        P(("expert", "replica"), None),
        P(("expert", "replica"), None),
        P("expert", "replica", None, None),
        P(None, "expert", None),
    )
    out_specs = (
        P("expert", "replica", None, None),
        P("replica", "expert", None),
        P(("expert", "replica"), None),
    )
    return jax.shard_map(
        per_device, mesh=mesh, in_specs=in_specs, out_specs=out_specs, check_vma=False
    )
```

```python
import functools
import math

import jax
import jax.numpy as jnp
from jax import lax
from jax.experimental import pallas as pl
from jax.experimental.pallas import tpu as pltpu
from jax.sharding import PartitionSpec as P

FIRST_PARTS = (7, 4, 3, 2)
SECOND_PARTS = (8, 4, 4)
BF16 = jnp.bfloat16
F32 = jnp.float32
MIB = 1024 * 1024
LITTLE = pl.CostEstimate(flops=1024, bytes_accessed=1024, transcendentals=0)


def info_of(offset, count):
    place, low, high = 0, 1, count // 2
    while high >= 1:
        place = place + (offset // high) % 2 * low
        low, high = low * 2, high // 2
    return place


def ring_place(index, count):
    return index // 2 if index % 2 == 0 else count - 1 - index // 2


def ring_index(place, count):
    return jnp.where(place < count // 2, 2 * place, 2 * (count - 1 - place) + 1)


def piece_of(source, place, count):
    ahead = (ring_place(source, count) + count - place) % count
    return jnp.where(ahead < count // 2, 2 * ahead, 2 * (count - ahead) - 1)


def source_of(piece, place, count):
    ahead = piece // 2 if piece % 2 == 0 else count - (piece + 1) // 2
    return ring_index((place + ahead) % count, count)


def turn_kernel(units, replicas, own_ref, grad_ref, *refs):
    outs, turned = refs[:-1], refs[-1]
    turned[...] = grad_ref[...].T
    rows = turned.shape[0] // replicas
    for out, parts in zip(outs, units):
        row = 0
        for flip, start, half in parts:
            for part in range(2):
                first = pl.multiple_of((own_ref[1] ^ (flip + part)) * rows + start, 128)
                out[row : row + half, :] = turned[pl.ds(first, half), :]
                row += half


def spread_kernel(
    count, own_ref, info_ref, hidden_ref, spread_ref, place_ref, gate_ref
):
    tokens, cap = spread_ref.shape[1], hidden_ref.shape[1] // count
    top = info_ref.shape[1] // 2
    me = own_ref[0]
    mine = me * pl.num_programs(0) + pl.program_id(0)
    masks, gates = [], []
    for source in range(count):
        info = info_ref[info_of(me ^ source, count)].astype(F32)
        same = info[:top].astype(jnp.int32) == mine
        masks.append(jnp.sum(jnp.where(same, 1.0, 0.0), axis=0, keepdims=True))
        gates.append(jnp.sum(jnp.where(same, info[top:], 0.0), axis=0, keepdims=True))
    mask, gate = jnp.concatenate(masks, axis=0), jnp.concatenate(gates, axis=0)
    before = lax.broadcasted_iota(jnp.int32, (tokens, tokens), 0)
    after = lax.broadcasted_iota(jnp.int32, (tokens, tokens), 1)
    earlier = jnp.where(before < after, 1.0, 0.0).astype(BF16)
    position = jnp.dot(mask.astype(BF16), earlier, preferred_element_type=F32)
    position = jnp.where(mask > 0.0, position, -1.0)
    base = lax.broadcasted_iota(jnp.int32, mask.shape, 0) * cap
    place_ref[0] = jnp.where(mask > 0.0, position.astype(jnp.int32) + base, -1)
    gate_ref[0] = gate
    turned = jnp.concatenate([position, gate], axis=0).T
    slot = lax.broadcasted_iota(jnp.int32, (tokens, cap), 1).astype(F32)
    for source in range(count):
        owns = turned[:, source : source + 1] == slot
        weights = jnp.where(owns, turned[:, count + source : count + source + 1], 0.0).astype(BF16)
        spread_ref[piece_of(source, own_ref[2], count)] = jnp.dot(
            weights, hidden_ref[0, source * cap : (source + 1) * cap, :], preferred_element_type=F32
        ).astype(BF16)


def down_kernel(first, count, *refs):
    piece_refs, spread_ref, outs, grads = refs[:count], refs[count], refs[count + 1 : -1], refs[-1]
    tokens, half = spread_ref.shape[1], grads.shape[0]

    @pl.when(pl.program_id(0) == 0)
    def _():
        for i, piece_ref in enumerate(piece_refs):
            grads[:, i * tokens : (i + 1) * tokens] = piece_ref[first : first + half, :]

    spread = spread_ref[...].reshape(count * tokens, spread_ref.shape[2])
    total = jnp.dot(grads[...], spread, preferred_element_type=F32)
    if outs[0].shape[0] == half and len(outs) > 1:
        total = total + outs[0][...].astype(F32)
        outs = outs[1:]
    row = 0
    for out in outs:
        out[...] = total[row : row + out.shape[0], :].astype(BF16)
        row += out.shape[0]


def up_kernel(units, replicas, count, own_ref, *refs):
    piece_refs, refs = refs[: len(units) * count], refs[len(units) * count :]
    weight_ref, place_ref, gate_ref, hidden_ref, hidden_grad_ref, slot_grad_ref, grads, placed = refs
    local, _, tokens = place_ref.shape
    slots = hidden_ref.shape[1]
    cap = slots // count
    group = 16 // math.gcd(cap, 16)
    rows = grads.shape[1] // replicas
    me, replica = own_ref[0], own_ref[1]
    expert = pl.program_id(0)

    def owned(x, low):
        slot = lax.broadcasted_iota(jnp.int32, (group * cap, tokens), 0) + low * cap
        return [place_ref[x, pl.ds(s, 1), :] == slot for s in range(low, low + group)]

    @pl.when(expert == 0)
    def _():
        for number, parts in enumerate(units):
            for i in range(count):
                turned = piece_refs[number * count + i][...].T
                token = pl.multiple_of(source_of(i, own_ref[2], count) * tokens, tokens)
                row = 0
                for flip, first, half in parts:
                    for part in range(2):
                        column = pl.multiple_of((replica ^ (flip + part)) * rows + first, 128)
                        grads[pl.ds(token, tokens), pl.ds(column, half)] = turned[:, row : row + half]
                        row += half
        for low in range(0, count, group):
            placing = jnp.concatenate(
                [
                    jnp.concatenate([jnp.where(o, 1.0, 0.0).astype(BF16) for o in owned(x, low)], axis=1)
                    for x in range(local)
                ],
                axis=0,
            )
            rows_there = jnp.dot(
                placing, grads[low * tokens : (low + group) * tokens, :], preferred_element_type=F32
            ).astype(BF16)
            for x in range(local):
                placed[x, low * cap : (low + group) * cap, :] = rows_there[
                    x * group * cap : (x + 1) * group * cap, :
                ]

    upstream = jnp.dot(placed[expert], weight_ref[0], preferred_element_type=F32)
    for low in range(0, count, group):
        slice_there = slice(low * cap, (low + group) * cap)
        mine = owned(expert, low)
        weighing = jnp.where(mine[0], gate_ref[expert, low : low + 1, :], 0.0)
        for s in range(1, group):
            weighing = weighing + jnp.where(mine[s], gate_ref[expert, low + s : low + s + 1, :], 0.0)
        gates = jnp.sum(weighing, axis=1, keepdims=True)
        part = upstream[slice_there, :]
        hidden_grad_ref[0, slice_there, :] = (gates * part).astype(BF16)
        slot_grad = jnp.sum(hidden_ref[0, slice_there, :].astype(F32) * part, axis=1, keepdims=True)
        for s in range(group):
            slot_grad_ref[0, pl.ds(me ^ (low + s), 1), :] = jnp.sum(
                jnp.where(mine[s], slot_grad, 0.0), axis=0, keepdims=True
            )


def join_kernel(near_ref, *refs):
    far_refs, out_ref = refs[: len(refs) - 1], refs[-1]
    local, width = out_ref.shape[1:]
    first = 0
    for far_ref in far_refs:
        if len(far_ref.shape) == 3:
            continue
        rows = pl.ds(first, far_ref.shape[0])
        total = near_ref[rows, :].astype(F32) + far_ref[...].astype(F32)
        for x in range(local):
            out_ref[rows, x, :] = total[:, x * width : (x + 1) * width].astype(BF16)
        first += far_ref.shape[0]


def tie(value, *others):
    return lax.optimization_barrier((value,) + others)[0]


SMEM = pl.BlockSpec(memory_space=pltpu.SMEM)


def whole(shape):
    return pl.BlockSpec(shape, lambda *_: (0,) * len(shape), pipeline_mode=pl.Buffered(1))


def vmem(shape):
    return pl.BlockSpec(shape, lambda *_: (0,) * len(shape))


def one_expert(*shape):
    return pl.BlockSpec((1,) + shape, lambda x: (x,) + (0,) * len(shape))


def per_device(grad_out, gates, experts, hidden, down_weight):
    count, replicas = lax.axis_size("expert"), lax.axis_size("replica")
    tokens, width = grad_out.shape
    top = experts.shape[1]
    local, _, slots, hidden_width = hidden.shape
    all_width = local * hidden_width
    room = min(max(2 * count, 16), 56)
    rows = width // replicas
    hidden = hidden.reshape(local, slots, hidden_width)
    me = lax.axis_index("expert")
    place = jnp.where(me % 2 == 0, me // 2, count - 1 - me // 2)
    own = jnp.stack([me, lax.axis_index("replica"), place]).astype(jnp.int32)

    share = rows // (sum(FIRST_PARTS) + sum(SECOND_PARTS))
    half, second = share * sum(FIRST_PARTS), share * sum(SECOND_PARTS)
    units = (((2, 0, half),), ((2, half, second), (0, 0, rows)))
    unit_shapes = [
        jax.ShapeDtypeStruct((sum(2 * part[2] for part in parts), tokens), BF16) for parts in units
    ]
    sent = pl.pallas_call(
        functools.partial(turn_kernel, units, replicas),
        out_shape=unit_shapes,
        in_specs=[SMEM, vmem(grad_out.shape)],
        out_specs=[vmem(s.shape) for s in unit_shapes],
        scratch_shapes=[pltpu.VMEM((width, tokens), BF16)],
        compiler_params=pltpu.CompilerParams(vmem_limit_bytes=56 * MIB),
        name="turn_tokens",
    )(own, grad_out)
    info = jnp.concatenate([experts.T.astype(BF16), gates.T], axis=0)

    flips = []
    while 2 ** len(flips) < count:
        flips.insert(0, 2 ** len(flips))

    def hop(held, flip):
        moved = lax.ppermute(held, "expert", [(i, i ^ flip) for i in range(count)])
        return jnp.concatenate([held, moved], axis=0)

    ring = [i for i in range(0, count, 2)] + [i for i in range(count - 1, 0, -2)]
    onward = [(ring[i], ring[(i + 1) % count]) for i in range(count)]
    backward = [(b, a) for a, b in onward]

    def turn_ring(pieces):
        right, left = pieces[-2:] if len(pieces) > 1 else pieces * 2
        moved = [lax.ppermute(right, "expert", onward)]
        if len(pieces) + 1 < count:
            moved.append(lax.ppermute(left, "expert", backward))
        return moved

    def spread_hidden(infos):
        return pl.pallas_call(
            functools.partial(spread_kernel, count),
            grid=(local,),
            out_shape=[
                jax.ShapeDtypeStruct((count, tokens, all_width), BF16),
                jax.ShapeDtypeStruct((local, count, tokens), jnp.int32),
                jax.ShapeDtypeStruct((local, count, tokens), F32),
            ],
            in_specs=[SMEM, whole(infos.shape), one_expert(slots, hidden_width)],
            out_specs=[
                pl.BlockSpec((count, tokens, hidden_width), lambda x: (0, 0, x)),
                one_expert(count, tokens),
                one_expert(count, tokens),
            ],
            compiler_params=pltpu.CompilerParams(vmem_limit_bytes=room * MIB),
            cost_estimate=LITTLE,
            name="spread_hidden",
        )(own, infos, hidden)

    def down(pieces, spread, first, half, parts=(1,), got=()):
        sizes = [half * part // sum(parts) for part in parts]

        def block(size):
            return pl.BlockSpec((size, hidden_width), lambda x: (0, x))

        return pl.pallas_call(
            functools.partial(down_kernel, first, count),
            grid=(local,),
            out_shape=[jax.ShapeDtypeStruct((size, all_width), BF16) for size in sizes],
            in_specs=[whole(piece.shape) for piece in pieces]
            + [pl.BlockSpec((count, tokens, hidden_width), lambda x: (0, 0, x))]
            + [block(half)] * len(got),
            out_specs=[block(size) for size in sizes],
            scratch_shapes=[pltpu.VMEM((half, count * tokens), BF16)],
            compiler_params=pltpu.CompilerParams(vmem_limit_bytes=room * MIB),
            cost_estimate=LITTLE,
            name="down_grad",
        )(*pieces, spread, *got)

    def to_mate(give):
        return lax.ppermute(give, "replica", [(i, i ^ 1) for i in range(replicas)])

    def to_far(value):
        return lax.ppermute(value, "replica", [(i, i ^ 2) for i in range(replicas)])

    def up(pieces, weight, place, gate):
        return pl.pallas_call(
            functools.partial(up_kernel, units, replicas, count),
            grid=(local,),
            out_shape=[
                jax.ShapeDtypeStruct(hidden.shape, BF16),
                jax.ShapeDtypeStruct((local, count, tokens), F32),
            ],
            in_specs=[SMEM]
            + [whole(piece.shape) for piece in pieces]
            + [
                one_expert(width, hidden_width),
                whole(place.shape),
                whole(gate.shape),
                one_expert(slots, hidden_width),
            ],
            out_specs=[one_expert(slots, hidden_width), one_expert(count, tokens)],
            scratch_shapes=[
                pltpu.VMEM((count * tokens, width), BF16),
                pltpu.VMEM((local, slots, width), BF16),
            ],
            compiler_params=pltpu.CompilerParams(vmem_limit_bytes=min(5 * count, 58) * MIB),
            cost_estimate=LITTLE,
            name="hidden_grad",
        )(own, *pieces, weight, place, gate, hidden)

    def join(near, fars, first, *before):
        block = sum(far.shape[0] for far in fars)
        return pl.pallas_call(
            join_kernel,
            grid=(1,),
            out_shape=jax.ShapeDtypeStruct((rows, local, hidden_width), BF16),
            in_specs=[pl.BlockSpec((block, all_width), lambda i: (first // block, 0))]
            + [vmem(far.shape) for far in fars]
            + [pl.BlockSpec(memory_space=pl.ANY)] * len(before),
            out_specs=pl.BlockSpec((block, local, hidden_width), lambda i: (first // block, 0, 0)),
            input_output_aliases={1 + len(fars): 0} if before else {},
            compiler_params=pltpu.CompilerParams(vmem_limit_bytes=24 * MIB),
            cost_estimate=LITTLE,
            name="join",
        )(near, *fars, *before)

    step = lax.optimization_barrier
    infos = tie(info, sent[0])[None]
    first, rest = [sent[0]], [sent[1]]
    for number in range(count // 2):
        moved = turn_ring(first)
        if number < len(flips):
            infos = hop(infos, flips[number])
        if number + 1 < count // 2:
            infos, rest[0], *first = step((infos, rest[0], *first, *moved))
        else:
            first = [*first, *moved]
    for flip in flips[count // 2 :]:
        infos = hop(infos, flip)
    spread, place, gate = spread_hidden(infos)
    spread, *first = step((spread, *first))

    def pass_on(returned, flip):
        stay = returned.reshape(count // (2 * flip), 2, flip, local, tokens)
        moved = lax.ppermute(stay[:, 1], "expert", [(i, i ^ flip) for i in range(count)])
        return jnp.stack([stay[:, 0], moved], axis=1).reshape(count, local, tokens)

    moved = turn_ring(rest)
    (give,) = down(first, spread, half, half)
    give, *rest = step((give, *rest, *moved))
    moved = turn_ring(rest)
    parts = list(down(first, spread, 0, half, FIRST_PARTS, (to_mate(give),)))
    *parts, spread = step((*parts, spread))
    rest = list(step((*rest, *moved)))
    weight = jnp.transpose(tie(down_weight, rest[-1]), (1, 0, 2))
    far_first = [to_far(part) for part in parts[:3]]
    moved = turn_ring(rest)
    far_first[0], weight, *rest = step((far_first[0], weight, *rest, *moved))
    while len(rest) < count:
        moved = turn_ring(rest)
        far_first[1], *rest = step((far_first[1], *rest, *moved))

    (give,) = down(rest, spread, second, second)
    far_first[2], give, spread, *parts = step((far_first[2], give, spread, *parts))
    far_first.append(to_far(parts[3]))
    (own_give,) = down(rest, spread, 2 * second + rows, rows)
    far_first[3], got, own_give, spread = step((far_first[3], to_mate(give), own_give, spread))
    sums = down(rest, spread, 0, second, SECOND_PARTS, (got,))
    (near,) = down(rest, tie(spread, *sums), 2 * second, rows, (1,), (to_mate(own_give),))
    near, place = step((near, place))
    far_second = [to_far(part) for part in sums]
    hidden_grad, slot_grad = up(first + rest, weight, place, gate)
    far_second[0], hidden_grad, slot_grad, near = step((far_second[0], hidden_grad, slot_grad, near))

    returned = pass_on(jnp.transpose(slot_grad, (1, 0, 2)), flips[0])
    down_grad = join(near, far_first, 0)
    far_second[1], returned, down_grad = step((far_second[1], returned, down_grad))
    returned = pass_on(returned, flips[1])
    down_grad = join(near, far_second[:1], half, down_grad)
    far_second[2], returned, down_grad = step((far_second[2], returned, down_grad))
    for flip in flips[2:]:
        returned = pass_on(returned, flip)
    sources = lax.axis_index("expert").astype(jnp.int32) ^ jnp.arange(count, dtype=jnp.int32)
    numbers = (sources[:, None] * local + jnp.arange(local, dtype=jnp.int32)[None]).reshape(-1)
    named = experts.T[:, None, :] == numbers[None, :, None]
    gate_grad = jnp.sum(jnp.where(named, returned.reshape(1, -1, tokens), 0.0), axis=1)
    gate_grad = gate_grad.T
    down_grad = join(near, far_second[1:], rows - sum(far.shape[0] for far in far_second[1:]), down_grad)
    return hidden_grad.reshape(local, 1, slots, hidden_width), down_grad, gate_grad


def solution(mesh):
    in_specs = (
        P(("expert", "replica"), None),
        P(("expert", "replica"), None),
        P(("expert", "replica"), None),
        P("expert", "replica", None, None),
        P(None, "expert", None),
    )
    out_specs = (
        P("expert", "replica", None, None),
        P("replica", "expert", None),
        P(("expert", "replica"), None),
    )
    return jax.shard_map(
        per_device, mesh=mesh, in_specs=in_specs, out_specs=out_specs, check_vma=False
    )
```
